32 devices in a mesh: ctx: 8 (over z, y), tp: 4 (over x, core).
Axes of the slice: x: 2, y: 2, z: 4, core: 2. Of those that a mesh axis runs over, the one named last changes fastest.
Arguments:
- tokens: float32 [4096, 1024], P(('ctx', 'tp')), may hold values from -6 to 6
- positions: int32 [4096], P('ctx'), may hold values from 0 to 4095, as said below
- q_weight: bfloat16 [1024, 2048], P('ctx', 'tp'), may hold values from -0.1875 to 0.1875
- k_weight: bfloat16 [1024, 1024], P('ctx', 'tp'), may hold values from -0.1875 to 0.1875
- v_weight: bfloat16 [1024, 1024], P('ctx', 'tp'), may hold values from -0.1875 to 0.1875
- o_weight: bfloat16 [2048, 1024], P('tp', 'ctx'), may hold values from -1.5 to 1.5
- gate_weight: bfloat16 [1024, 3072], P('ctx', 'tp'), may hold values from -0.1875 to 0.1875
- up_weight: bfloat16 [1024, 3072], P('ctx', 'tp'), may hold values from -0.1875 to 0.1875
- down_weight: bfloat16 [3072, 1024], P('tp', 'ctx'), may hold values from -0.109375 to 0.109375
- norm1_gain: float32 [1024], replicated, may hold values from 0.5 to 1.5
- norm2_gain: float32 [1024], replicated, may hold values from 0.5 to 1.5
- q_gain: float32 [128], replicated, may hold values from 0.5 to 1.6
- k_gain: float32 [128], replicated, may hold values from 0.5 to 1.6
- cotangent: float32 [4096, 1024], P(('ctx', 'tp')), may hold values from -6 to 6
Outputs:
- block_out: float32 [4096, 1024], P(('ctx', 'tp'))
- input_grad: float32 [4096, 1024], P(('ctx', 'tp'))
- q_weight_grad: float32 [1024, 2048], P('ctx', 'tp')
- k_weight_grad: float32 [1024, 1024], P('ctx', 'tp')
- v_weight_grad: float32 [1024, 1024], P('ctx', 'tp')
- o_weight_grad: float32 [2048, 1024], P('tp', 'ctx')
- gate_weight_grad: float32 [1024, 3072], P('ctx', 'tp')
- up_weight_grad: float32 [1024, 3072], P('ctx', 'tp')
- down_weight_grad: float32 [3072, 1024], P('tp', 'ctx')
- norm1_grad: float32 [1024], replicated
- norm2_grad: float32 [1024], replicated
- q_gain_grad: float32 [128], replicated
- k_gain_grad: float32 [128], replicated
The draws below stay inside these ranges and needn't reach their ends.
Inputs may be any that keep to these rules, and one draw needn't show every extreme that they name: Each aligned block of 512 rows holds the positions b * 512 + i for i = 0 to 511 in order, for a block number b; every block number 0 to 7 occurs once.
All inputs are finite; a program needn't handle non-finite values.
Results may differ from the reference program's by a relative error of at most 0.022.
Values may be sent and summed in bfloat16 or wider, within the bound.
A program may use at most 192 MiB of HBM per device.

```python
import jax
import jax.numpy as jnp
from jax import lax

D = 1024
HQ = 16
KV = 8
HD = 128
FF = 3072
TOK_DEV = 512
DOCS = 2
SEQ = 4096
BLOCKS = 8


def draw_positions(key, part):
    order = jax.random.permutation(key, BLOCKS).astype(jnp.int32)
    offsets = jnp.arange(TOK_DEV, dtype=jnp.int32)
    return (order[:, None] * TOK_DEV + offsets[None, :]).reshape(SEQ).astype(jnp.int32)


def draw_gain_table(key):
    return jax.random.uniform(key, (HD,), jnp.float32, 0.5, 1.6)


def draw_q_gain(key, part):
    return draw_gain_table(jax.random.fold_in(key, 11))


def draw_k_gain(key, part):
    return draw_gain_table(jax.random.fold_in(key, 23))


def strengthened(entries, rng, source, target, parts, factor):
    def block_of(axis_at):
        return (jnp.arange(entries.shape[axis_at]) // (entries.shape[axis_at] // parts)).reshape((-1,) + (1,) * (entries.ndim - 1 - axis_at))

    near = jax.random.permutation(rng, parts)[block_of(target)]
    far = (block_of(target) + parts // 2) % parts
    return jnp.where((block_of(source) == near) | (block_of(source) == far), factor * entries, entries)


def shard_levels(key, extent, split, least, largest):
    def one(position, parts):
        steps = jax.random.uniform(jax.random.fold_in(jax.random.fold_in(key, 6), position), (parts,), jnp.float32, least / len(split), largest / len(split))
        return jnp.repeat(jnp.exp(steps), extent[position] // parts).reshape((-1,) + (1,) * (len(extent) - position - 1))

    loudness = one(*split[0])
    for cut in split[1:]:
        loudness = loudness * one(*cut)
    return loudness


def centred(own_key, shape, spread, bound, cuts=(), kind=jnp.bfloat16):
    gain = shard_levels(own_key, shape, cuts, -0.22, 0.18) if cuts else 1.0
    drawn = jax.random.normal(own_key, shape, jnp.float32) * spread * gain
    return jnp.minimum(jnp.maximum(drawn, -bound), bound).astype(kind)


def gaussian_with(stream_key, shape, scale, reach, shards, heavy, kind=jnp.bfloat16):
    values = scale * jax.random.normal(stream_key, shape, jnp.float32)
    if shards:
        values = values * shard_levels(stream_key, shape, shards, -0.22, 0.18)
    return jnp.clip(strengthened(values, jax.random.fold_in(stream_key, 3), *heavy), -reach, reach).astype(kind)


def setup_inputs(seed: int = 0) -> dict:
    splits = jax.random.split(jax.random.key(seed), 15)
    tokens = gaussian_with(splits[0], (SEQ, D), 1.0, 6.0, ((0, 32),), (0, 1, 32, 2.75), jnp.float32)
    positions = draw_positions(jax.random.fold_in(splits[14], 71), 0)
    q_weight = centred(splits[2], (D, HQ * HD), D ** -0.5, 0.1875, ((0, 8), (1, 4)))
    k_weight = centred(splits[3], (D, KV * HD), D ** -0.5, 0.1875, ((0, 8), (1, 4)))
    v_weight = centred(splits[4], (D, KV * HD), D ** -0.5, 0.1875, ((0, 8), (1, 4)))
    o_weight = centred(splits[5], (HQ * HD, D), 16 ** -0.5, 1.5, ((0, 4), (1, 8)))
    gate_weight = centred(splits[6], (D, FF), D ** -0.5, 0.1875, ((0, 8), (1, 4)))
    up_weight = centred(splits[7], (D, FF), D ** -0.5, 0.1875, ((0, 8), (1, 4)))
    down_weight = centred(splits[8], (FF, D), FF ** -0.5, 0.109375, ((0, 4), (1, 8)))
    norm1_gain = jnp.clip(1.0 + 0.1 * jax.random.normal(splits[9], (D,), jnp.float32), 0.5, 1.5)
    norm2_gain = jnp.clip(1.0 + 0.1 * jax.random.normal(splits[10], (D,), jnp.float32), 0.5, 1.5)
    q_gain = draw_q_gain(jax.random.fold_in(splits[14], 71), 0)
    k_gain = draw_k_gain(jax.random.fold_in(splits[14], 71), 0)
    cotangent = gaussian_with(splits[13], (SEQ, D), 1.0, 6.0, ((0, 32),), (0, 1, 32, 2.75), jnp.float32)
    return dict(tokens=tokens, positions=positions, q_weight=q_weight, k_weight=k_weight, v_weight=v_weight, o_weight=o_weight, gate_weight=gate_weight, up_weight=up_weight, down_weight=down_weight, norm1_gain=norm1_gain, norm2_gain=norm2_gain, q_gain=q_gain, k_gain=k_gain, cotangent=cotangent)


EPSILON = 1e-06
ROPE_BASE = 1000000.0
MASKED = -1e+30

def inv_rms(values):
    return lax.rsqrt(lax.optimization_barrier(jnp.mean(values * values, axis=-1, keepdims=True)) + EPSILON)

def narrow(values):
    return lax.optimization_barrier(values.astype(jnp.bfloat16)).astype(jnp.float32)

def rope_tables(positions, width):
    half_width = width // 2
    inverse = ROPE_BASE ** (-(jnp.arange(half_width, dtype=jnp.float32) * 2.0) / width)
    angles = positions.astype(jnp.float32)[:, None] * inverse[None, :]
    return (jnp.cos(angles), jnp.sin(angles))

def spread_table(table, values):
    half_width = values.shape[-1] // 2
    table_shape = (table.shape[0],) + (1,) * (values.ndim - 2) + (half_width,)
    return table.reshape(table_shape)

def rotate(values, cosine, sine_table):
    half_width = values.shape[-1] // 2
    cosine = spread_table(cosine, values)
    sine_table = spread_table(sine_table, values)
    former = values[..., :half_width]
    latter = values[..., half_width:]
    return jnp.concatenate([former * cosine - latter * sine_table, latter * cosine + former * sine_table], axis=-1)

def rotate_back(grads, cosine, sine_table):
    half_width = grads.shape[-1] // 2
    cosine = spread_table(cosine, grads)
    sine_table = spread_table(sine_table, grads)
    former = grads[..., :half_width]
    latter = grads[..., half_width:]
    return jnp.concatenate([former * cosine + latter * sine_table, latter * cosine - former * sine_table], axis=-1)

def norm_back(upstream, normed, inverse):
    return inverse * (upstream - normed * lax.optimization_barrier(jnp.mean(upstream * normed, axis=-1, keepdims=True)))

def reference(tokens, positions, q_weight, k_weight, v_weight, o_weight, gate_weight, up_weight, down_weight, norm1_gain, norm2_gain, q_gain, k_gain, cotangent):
    seq_len = tokens.shape[0]
    doc_len = seq_len // DOCS
    group_size = HQ // KV
    score_scale = HD ** (-0.5)
    block_len = min(512, seq_len)
    block_count = seq_len // block_len
    inv_first = inv_rms(tokens)
    normed_first = tokens * inv_first
    hidden_first = (normed_first * norm1_gain).astype(jnp.bfloat16)
    local_pos = (positions % doc_len).astype(jnp.int32)
    doc_starts = (positions - local_pos).astype(jnp.int32)
    cosine, sine_table = rope_tables(local_pos, HD)
    query_raw = jnp.dot(hidden_first, q_weight, preferred_element_type=jnp.float32).reshape(seq_len, KV, group_size, HD)
    key_raw = jnp.dot(hidden_first, k_weight, preferred_element_type=jnp.float32).reshape(seq_len, KV, HD)
    values = jnp.dot(hidden_first, v_weight, preferred_element_type=jnp.float32).astype(jnp.bfloat16).reshape(seq_len, KV, HD)
    inv_query = inv_rms(query_raw)
    query_hat = query_raw * inv_query
    queries = rotate(query_hat * q_gain, cosine, sine_table).astype(jnp.bfloat16)
    inv_key = inv_rms(key_raw)
    key_hat = key_raw * inv_key
    keys_low = rotate(key_hat * k_gain, cosine, sine_table).astype(jnp.bfloat16)
    keys_wide = keys_low.astype(jnp.float32)
    values_wide = values.astype(jnp.float32)
    query_blocks = queries.reshape(block_count, block_len, KV, group_size, HD)
    position_blocks = positions.reshape(block_count, block_len)
    start_blocks = doc_starts.reshape(block_count, block_len)

    def allowed_of(query_pos, query_start):
        key_row = positions[None, None, None, :]
        return jnp.logical_and(key_row <= query_pos[None, None, :, None], key_row >= query_start[None, None, :, None])

    def forward_block(inputs):
        query_part, query_pos, query_start = inputs
        scores = jnp.einsum('qgjd,kgd->gjqk', query_part.astype(jnp.float32), keys_wide) * score_scale
        allowed = allowed_of(query_pos, query_start)
        scores = jnp.where(allowed, scores, MASKED)
        row_top = lax.optimization_barrier(jnp.max(scores, axis=-1))
        probs = jnp.where(allowed, jnp.exp(scores - row_top[..., None]), 0.0)
        row_total = lax.optimization_barrier(jnp.sum(probs, axis=-1))
        mixed_sum = jnp.einsum('gjqk,kgd->qgjd', narrow(probs), values_wide)
        result = mixed_sum / jnp.transpose(row_total, (2, 0, 1))[..., None]
        return (result.astype(jnp.bfloat16), row_top + jnp.log(row_total))
    attended, log_totals = lax.map(forward_block, (query_blocks, position_blocks, start_blocks))
    attended_flat = attended.reshape(seq_len, HQ * HD)
    middle = tokens + jnp.dot(attended_flat, o_weight, preferred_element_type=jnp.float32)
    inv_second = inv_rms(middle)
    normed_second = middle * inv_second
    hidden_second = (normed_second * norm2_gain).astype(jnp.bfloat16)
    gate = jnp.dot(hidden_second, gate_weight, preferred_element_type=jnp.float32)
    up_proj = jnp.dot(hidden_second, up_weight, preferred_element_type=jnp.float32)
    sigmoid = jax.nn.sigmoid(gate)
    activation = (gate * sigmoid * up_proj).astype(jnp.bfloat16)
    block_out = middle + jnp.dot(activation, down_weight, preferred_element_type=jnp.float32)
    cot_low = cotangent.astype(jnp.bfloat16)
    act_grad = jnp.dot(cot_low, down_weight.T, preferred_element_type=jnp.float32)
    down_weight_grad = jnp.dot(activation.T, cot_low, preferred_element_type=jnp.float32)
    gate_grad = (act_grad * up_proj * sigmoid * (1.0 + gate * (1.0 - sigmoid))).astype(jnp.bfloat16)
    up_grad = (act_grad * gate * sigmoid).astype(jnp.bfloat16)
    hidden2_grad = jnp.dot(gate_grad, gate_weight.T, preferred_element_type=jnp.float32) + jnp.dot(up_grad, up_weight.T, preferred_element_type=jnp.float32)
    gate_weight_grad = jnp.dot(hidden_second.T, gate_grad, preferred_element_type=jnp.float32)
    up_weight_grad = jnp.dot(hidden_second.T, up_grad, preferred_element_type=jnp.float32)
    norm2_grad = lax.optimization_barrier(jnp.sum(hidden2_grad * normed_second, axis=0))
    middle_grad = norm_back(hidden2_grad * norm2_gain, normed_second, inv_second) + cotangent
    mid_low = middle_grad.astype(jnp.bfloat16)
    attended_grad = jnp.dot(mid_low, o_weight.T, preferred_element_type=jnp.float32).astype(jnp.bfloat16)
    o_weight_grad = jnp.dot(attended_flat.T, mid_low, preferred_element_type=jnp.float32)
    grad_blocks = attended_grad.reshape(block_count, block_len, KV, group_size, HD)
    delta_rows = lax.optimization_barrier(jnp.sum(attended_grad.astype(jnp.float32).reshape(seq_len, KV, group_size, HD) * attended.reshape(seq_len, KV, group_size, HD).astype(jnp.float32), axis=-1))
    delta_blocks = delta_rows.reshape(block_count, block_len, KV, group_size)

    def backward_block(carried, inputs):
        key_acc, value_acc = carried
        query_part, query_pos, query_start, grad_part, delta_part, log_part = inputs
        query_wide = query_part.astype(jnp.float32)
        grad_wide = grad_part.astype(jnp.float32)
        scores = jnp.einsum('qgjd,kgd->gjqk', query_wide, keys_wide) * score_scale
        allowed = allowed_of(query_pos, query_start)
        probs = jnp.where(allowed, jnp.exp(scores - log_part[..., None]), 0.0)
        prob_grad = jnp.einsum('qgjd,kgd->gjqk', grad_wide, values_wide)
        score_grad = probs * (prob_grad - jnp.transpose(delta_part, (1, 2, 0))[..., None])
        probs_low = narrow(probs)
        score_low = narrow(score_grad)
        value_acc = value_acc + jnp.einsum('gjqk,qgjd->kgd', probs_low, grad_wide)
        key_acc = key_acc + jnp.einsum('gjqk,qgjd->kgd', score_low, query_wide) * score_scale
        query_grad = jnp.einsum('gjqk,kgd->qgjd', score_low, keys_wide) * score_scale
        return ((key_acc, value_acc), query_grad)
    zeros_kv = jnp.zeros((seq_len, KV, HD), jnp.float32)
    (key_grad, value_grad), query_grads = lax.scan(backward_block, (zeros_kv, zeros_kv), (query_blocks, position_blocks, start_blocks, grad_blocks, delta_blocks, log_totals))
    query_grad = query_grads.reshape(seq_len, KV, group_size, HD)
    query_back = rotate_back(query_grad, cosine, sine_table)
    q_gain_grad = lax.optimization_barrier(jnp.sum(query_back * query_hat, axis=(0, 1, 2)))
    query_raw_grad = norm_back(query_back * q_gain, query_hat, inv_query).astype(jnp.bfloat16).reshape(seq_len, HQ * HD)
    key_back = rotate_back(key_grad, cosine, sine_table)
    k_gain_grad = lax.optimization_barrier(jnp.sum(key_back * key_hat, axis=(0, 1)))
    key_raw_grad = norm_back(key_back * k_gain, key_hat, inv_key).astype(jnp.bfloat16).reshape(seq_len, KV * HD)
    value_low = value_grad.astype(jnp.bfloat16).reshape(seq_len, KV * HD)
    hidden1_grad = jnp.dot(query_raw_grad, q_weight.T, preferred_element_type=jnp.float32)
    hidden1_grad = hidden1_grad + jnp.dot(key_raw_grad, k_weight.T, preferred_element_type=jnp.float32)
    hidden1_grad = hidden1_grad + jnp.dot(value_low, v_weight.T, preferred_element_type=jnp.float32)
    q_weight_grad = jnp.dot(hidden_first.T, query_raw_grad, preferred_element_type=jnp.float32)
    k_weight_grad = jnp.dot(hidden_first.T, key_raw_grad, preferred_element_type=jnp.float32)
    v_weight_grad = jnp.dot(hidden_first.T, value_low, preferred_element_type=jnp.float32)
    norm1_grad = lax.optimization_barrier(jnp.sum(hidden1_grad * normed_first, axis=0))
    input_grad = norm_back(hidden1_grad * norm1_gain, normed_first, inv_first) + middle_grad
    return (block_out, input_grad, q_weight_grad, k_weight_grad, v_weight_grad, o_weight_grad, gate_weight_grad, up_weight_grad, down_weight_grad, norm1_grad, norm2_grad, q_gain_grad, k_gain_grad)
```

```python
import functools
import math

import jax
import jax.numpy as jnp
from jax import lax
from jax.experimental import pallas as pl
from jax.experimental.pallas import tpu as pltpu
from jax.sharding import PartitionSpec as P

DOCS = 2


EPSILON = 1e-06
ROPE_BASE = 1000000.0
MASKED = -1e30
KEY_SPAN = 512
MESH = pl.DeviceIdType.MESH


def inv_rms(values):
    return lax.rsqrt(jnp.mean(values * values, axis=-1, keepdims=True) + EPSILON)


def rope_tables(positions, width):
    half_width = width // 2
    inverse = ROPE_BASE ** (-(jnp.arange(half_width, dtype=jnp.float32) * 2.0) / width)
    angles = positions.astype(jnp.float32)[:, None] * inverse[None, :]
    return (jnp.cos(angles), jnp.sin(angles))


def spread_table(table, values):
    half_width = values.shape[-1] // 2
    table_shape = (table.shape[0],) + (1,) * (values.ndim - 2) + (half_width,)
    return table.reshape(table_shape)


def rotate(values, cosine, sine_table):
    half_width = values.shape[-1] // 2
    cosine = spread_table(cosine, values)
    sine_table = spread_table(sine_table, values)
    former = values[..., :half_width]
    latter = values[..., half_width:]
    return jnp.concatenate(
        [former * cosine - latter * sine_table, latter * cosine + former * sine_table], axis=-1
    )


def rotate_back(grads, cosine, sine_table):
    half_width = grads.shape[-1] // 2
    cosine = spread_table(cosine, grads)
    sine_table = spread_table(sine_table, grads)
    former = grads[..., :half_width]
    latter = grads[..., half_width:]
    return jnp.concatenate(
        [former * cosine + latter * sine_table, latter * cosine - former * sine_table], axis=-1
    )


def norm_back(upstream, normed, inverse):
    return inverse * (upstream - normed * jnp.mean(upstream * normed, axis=-1, keepdims=True))


def contract_last(operand_left, operand_right):
    return lax.dot_general(
        operand_left, operand_right, (((1,), (1,)), ((), ())), preferred_element_type=jnp.float32
    )


def contract_rows(operand_left, operand_right):
    return lax.dot_general(
        operand_left, operand_right, (((0,), (0,)), ((), ())), preferred_element_type=jnp.float32
    )


def exchange_kernel(axis, n, gather_count, scatter_count, *refs):
    half = n // 2
    position = 0

    def take(count):
        nonlocal position
        taken = refs[position : position + count]
        position += count
        return taken

    shards, parts = take(gather_count), take(scatter_count)
    wholes, totals = take(gather_count), take(scatter_count)
    from_pair, from_peer = take(scatter_count), take(scatter_count)
    gather_sems = take(5) if gather_count else None
    scatter_sems = take(4) if scatter_count else None

    me = lax.axis_index(axis)
    parity = lax.rem(me, 2)
    group = me // 2
    pair = me + 1 - 2 * parity

    def peer(shift):
        return lax.rem(group + shift, half) * 2 + parity

    barrier = pltpu.get_barrier_semaphore()
    for other in [pair] + [peer(shift) for shift in range(1, half)]:
        pl.semaphore_signal(barrier, inc=1, device_id={axis: other}, device_id_type=MESH)
    pl.semaphore_wait(barrier, half)

    def push(source, target, send, receive, other):
        return pltpu.make_async_remote_copy(
            src_ref=source,
            dst_ref=target,
            send_sem=send,
            recv_sem=receive,
            device_id={axis: other},
            device_id_type=MESH,
        )

    pending = []
    first = {}
    for index in range(scatter_count):
        send_pair, recv_pair, send_peer, recv_peer = scatter_sems
        for shift in list(range(1, half)) + [0]:
            wanted = lax.rem(group + shift, half) * 2 + 1 - parity
            first[index, shift] = push(
                parts[index].at[wanted],
                from_pair[index].at[shift],
                send_pair.at[index, shift],
                recv_pair.at[index, shift],
                pair,
            )
            first[index, shift].start()
    direct = {}
    for index in range(gather_count):
        own_sem, send_peer_g, recv_peer_g, send_pair_g, recv_pair_g = gather_sems
        own = pltpu.make_async_copy(shards[index], wholes[index].at[me], own_sem.at[index])
        own.start()
        pending.append(own.wait)
        for shift in range(1, half):
            direct[index, shift] = push(
                shards[index],
                wholes[index].at[me],
                send_peer_g.at[index, shift],
                recv_peer_g.at[index, shift],
                peer(shift),
            )
            direct[index, shift].start()
        across = push(
            shards[index],
            wholes[index].at[me],
            send_pair_g.at[index, 0],
            recv_pair_g.at[index, 0],
            pair,
        )
        across.start()
        pending.append(across.wait)
    second = {}
    for index in range(scatter_count):
        rows = parts[index].shape[1]
        chunk = min(rows, 32)
        for shift in list(range(1, half)) + [0]:
            first[index, shift].wait_recv()
            kept = peer(shift)

            def add_pair(step, unused, index=index, shift=shift, kept=kept, chunk=chunk):
                span = pl.ds(pl.multiple_of(step * chunk, chunk), chunk)
                summed = parts[index][kept, span, :].astype(jnp.float32) + from_pair[index][
                    shift, span, :
                ].astype(jnp.float32)
                if shift:
                    from_pair[index][shift, span, :] = summed.astype(jnp.bfloat16)
                else:
                    totals[index][span, :] = summed
                return unused

            lax.fori_loop(0, rows // chunk, add_pair, 0)
            if shift:
                second[index, shift] = push(
                    from_pair[index].at[shift],
                    from_peer[index].at[shift - 1],
                    send_peer.at[index, shift],
                    recv_peer.at[index, shift],
                    peer(shift),
                )
                second[index, shift].start()
    for index in range(gather_count):
        for shift in range(1, half):
            direct[index, shift].wait_recv()
            origin = lax.rem(group + half - shift, half) * 2 + parity
            onward = push(
                wholes[index].at[origin],
                wholes[index].at[origin],
                send_pair_g.at[index, shift],
                recv_pair_g.at[index, shift],
                pair,
            )
            onward.start()
            pending.append(direct[index, shift].wait_send)
            pending.append(onward.wait)
    for index in range(scatter_count):
        rows = parts[index].shape[1]
        chunk = min(rows, 32)
        for shift in range(1, half):
            second[index, shift].wait_recv()

        def add_peers(step, unused, index=index, chunk=chunk):
            span = pl.ds(pl.multiple_of(step * chunk, chunk), chunk)
            summed = totals[index][span, :]
            for shift in range(1, half):
                summed += from_peer[index][shift - 1, span, :].astype(jnp.float32)
            totals[index][span, :] = summed
            return unused

        lax.fori_loop(0, rows // chunk, add_peers, 0)
        for shift in range(half):
            pending.append(first[index, shift].wait_send)
            if shift:
                pending.append(second[index, shift].wait_send)
    for wait in pending:
        wait()


def exchange(axis, gathers, scatters, number):
    n = lax.axis_size(axis)
    half = n // 2
    split = [part.reshape((n, part.shape[0] // n) + part.shape[1:]) for part in scatters]
    anywhere = pl.BlockSpec(memory_space=pl.ANY)
    vmem = pl.BlockSpec(memory_space=pltpu.VMEM)
    dma = pltpu.SemaphoreType.DMA
    scratch = [pltpu.VMEM((half,) + part.shape[1:], part.dtype) for part in split]
    scratch += [pltpu.VMEM((half - 1,) + part.shape[1:], part.dtype) for part in split]
    if gathers:
        scratch += [dma((len(gathers),))] + [dma((len(gathers), half))] * 4
    if scatters:
        scratch += [dma((len(scatters), half))] * 4
    results = pl.pallas_call(
        functools.partial(exchange_kernel, axis, n, len(gathers), len(scatters)),
        out_shape=[jax.ShapeDtypeStruct((n,) + shard.shape, shard.dtype) for shard in gathers]
        + [jax.ShapeDtypeStruct(part.shape[1:], jnp.float32) for part in split],
        in_specs=[anywhere] * len(gathers) + [vmem] * len(split),
        out_specs=[anywhere] * len(gathers) + [vmem] * len(split),
        scratch_shapes=scratch,
        compiler_params=pltpu.CompilerParams(
            collective_id=number,
            has_side_effects=True,
            vmem_limit_bytes=(48 if scatters else 4) * 1024 * 1024,
        ),
    )(*gathers, *split)
    count = len(gathers)
    return [
        whole.reshape((n * shard.shape[0],) + shard.shape[1:])
        for whole, shard in zip(results[:count], gathers)
    ] + list(results[count:])


def step_length(length):
    return math.gcd(length, KEY_SPAN)


def allowed_mask(key_pos, query_pos, query_start):
    key_row = key_pos[None, None, None, :]
    return jnp.logical_and(
        key_row <= query_pos[None, None, :, None], key_row >= query_start[None, None, :, None]
    )


def outside(key_pos, query_pos, query_start):
    return jnp.logical_or(
        jnp.min(key_pos) > jnp.max(query_pos), jnp.max(key_pos) < jnp.min(query_start)
    )


def attend_block(
    carried, keys_part, values_part, key_pos, queries, query_pos, query_start, score_scale
):

    def attend_work(current):
        row_top, row_total, mixed_sum = current
        scores = (
            jnp.einsum("qgjd,kgd->gjqk", queries, keys_part, preferred_element_type=jnp.float32)
            * score_scale
        )
        allowed = allowed_mask(key_pos, query_pos, query_start)
        scores = jnp.where(allowed, scores, MASKED)
        new_top = jnp.maximum(row_top, jnp.max(scores, axis=-1))
        probs = jnp.where(allowed, jnp.exp(scores - new_top[..., None]), 0.0)
        factor = jnp.exp(row_top - new_top)
        row_total = row_total * factor + jnp.sum(probs, axis=-1)
        update = jnp.einsum(
            "gjqk,kgd->qgjd",
            probs.astype(jnp.bfloat16),
            values_part,
            preferred_element_type=jnp.float32,
        )
        mixed_sum = mixed_sum * jnp.transpose(factor, (2, 0, 1))[..., None] + update
        return (new_top, row_total, mixed_sum)

    return lax.cond(
        outside(key_pos, query_pos, query_start), lambda current: current, attend_work, carried
    )


def sweep_keys(
    carried, keys_part, values_part, key_pos, queries, query_pos, query_start, score_scale
):
    length = keys_part.shape[0]
    step_len = step_length(length)
    step_count = length // step_len

    def sweep_step(current, pieces):
        return (
            attend_block(
                current,
                pieces[0],
                pieces[1],
                pieces[2],
                queries,
                query_pos,
                query_start,
                score_scale,
            ),
            None,
        )

    stacked = (
        keys_part.reshape((step_count, step_len) + keys_part.shape[1:]),
        values_part.reshape((step_count, step_len) + values_part.shape[1:]),
        key_pos.reshape(step_count, step_len),
    )
    carried, unused = lax.scan(sweep_step, carried, stacked)
    return carried


def score_pair(keys_part, values_part, key_pos, query_side):
    queries, query_pos, query_start, grad_out, delta_rows, log_total, score_scale = query_side
    scores = (
        jnp.einsum("qgjd,kgd->gjqk", queries, keys_part, preferred_element_type=jnp.float32)
        * score_scale
    )
    allowed = allowed_mask(key_pos, query_pos, query_start)
    probs = jnp.where(allowed, jnp.exp(scores - log_total[..., None]), 0.0)
    prob_grad = jnp.einsum(
        "qgjd,kgd->gjqk", grad_out, values_part, preferred_element_type=jnp.float32
    )
    score_grad = probs * (prob_grad - delta_rows[..., None])
    return (probs.astype(jnp.bfloat16), score_grad.astype(jnp.bfloat16))


def stack_steps(all_keys, all_values, all_pos):
    length = all_keys.shape[0]
    step_len = step_length(length)
    step_count = length // step_len
    return (
        all_keys.reshape((step_count, step_len) + all_keys.shape[1:]),
        all_values.reshape((step_count, step_len) + all_values.shape[1:]),
        all_pos.reshape(step_count, step_len),
    )


def attend_back(all_keys, all_values, all_pos, query_side, span_rows):
    queries, query_pos, query_start, grad_out, delta_rows, log_total, score_scale = query_side

    def grad_step(current, pieces):
        keys_part, values_part, key_pos = pieces

        def grad_work(query_acc):
            probs_low, score_low = score_pair(keys_part, values_part, key_pos, query_side)
            query_part = jnp.einsum(
                "gjqk,kgd->qgjd", score_low, keys_part, preferred_element_type=jnp.float32
            )
            value_part = jnp.einsum(
                "gjqk,qgjd->kgd", probs_low, grad_out, preferred_element_type=jnp.float32
            )
            key_part = (
                jnp.einsum("gjqk,qgjd->kgd", score_low, queries, preferred_element_type=jnp.float32)
                * score_scale
            )
            return (
                query_acc + query_part * score_scale,
                jnp.stack([key_part, value_part], axis=1).astype(jnp.bfloat16),
            )

        def skipped(query_acc):
            return (
                query_acc,
                jnp.zeros((keys_part.shape[0], 2) + keys_part.shape[1:], jnp.bfloat16),
            )

        return lax.cond(outside(key_pos, query_pos, query_start), skipped, grad_work, current)

    initial = jnp.zeros(queries.shape, jnp.float32)
    query_grad, terms = lax.scan(grad_step, initial, stack_steps(all_keys, all_values, all_pos))
    return query_grad, terms.reshape(span_rows, -1)


def local(
    tokens,
    positions,
    q_weight,
    k_weight,
    v_weight,
    o_weight,
    gate_weight,
    up_weight,
    down_weight,
    norm1_gain,
    norm2_gain,
    q_gain,
    k_gain,
    cotangent,
):
    head_width = q_gain.shape[0]
    score_scale = head_width ** (-0.5)
    local_heads = q_weight.shape[1] // head_width
    local_groups = k_weight.shape[1] // head_width
    group_size = local_heads // local_groups
    doc_len = positions.shape[0] * lax.axis_size("ctx") // DOCS
    qkv_shard = jnp.concatenate([q_weight, k_weight, v_weight], axis=1)
    pair_shard = jnp.concatenate([gate_weight, up_weight], axis=1)
    inv_first = inv_rms(tokens)
    normed_first = tokens * inv_first
    hidden_first, cot_low = exchange(
        "tp",
        [(normed_first * norm1_gain).astype(jnp.bfloat16), cotangent.astype(jnp.bfloat16)],
        [],
        0,
    )
    block_len = hidden_first.shape[0]
    qkv_full, wo_turned, pair_full, wd_turned, all_pos = exchange(
        "ctx",
        [qkv_shard, o_weight.T, pair_shard, down_weight.T, positions.reshape(-1, 128)],
        [],
        1,
    )
    all_pos = all_pos.reshape(-1)
    local_pos = positions % doc_len
    query_start = positions - local_pos
    cosine, sine_table = rope_tables(local_pos, head_width)
    query_width = local_heads * head_width
    key_width = local_groups * head_width
    raw = jnp.dot(hidden_first, qkv_full, preferred_element_type=jnp.float32)
    query_raw = raw[:, :query_width].reshape(block_len, local_groups, group_size, head_width)
    key_raw = raw[:, query_width : query_width + key_width].reshape(
        block_len, local_groups, head_width
    )
    values_local = raw[:, query_width + key_width :].astype(jnp.bfloat16)
    inv_query = inv_rms(query_raw)
    query_hat = query_raw * inv_query
    queries = rotate(query_hat * q_gain, cosine, sine_table).astype(jnp.bfloat16)
    inv_key = inv_rms(key_raw)
    key_hat = key_raw * inv_key
    keys_local = rotate(key_hat * k_gain, cosine, sine_table).astype(jnp.bfloat16)
    initial = (
        jnp.full((local_groups, group_size, block_len), MASKED, jnp.float32),
        jnp.zeros((local_groups, group_size, block_len), jnp.float32),
        jnp.zeros((block_len, local_groups, group_size, head_width), jnp.float32),
    )
    all_keys, all_values = exchange(
        "ctx", [keys_local.reshape(block_len, key_width), values_local], [], 2
    )
    all_keys = all_keys.reshape(-1, local_groups, head_width)
    all_values = all_values.reshape(-1, local_groups, head_width)
    row_top, row_total, mixed_sum = sweep_keys(
        initial, all_keys, all_values, all_pos, queries, positions, query_start, score_scale
    )
    attended = (mixed_sum / jnp.transpose(row_total, (2, 0, 1))[..., None]).astype(jnp.bfloat16)
    log_total = row_top + jnp.log(row_total)
    attended_flat = attended.reshape(block_len, query_width)
    (projected,) = exchange(
        "tp", [], [contract_last(attended_flat, wo_turned).astype(jnp.bfloat16)], 3
    )
    middle = tokens + projected
    inv_second = inv_rms(middle)
    normed_second = middle * inv_second
    (hidden_second,) = exchange(
        "tp", [(normed_second * norm2_gain).astype(jnp.bfloat16)], [], 4
    )
    unit_count = gate_weight.shape[1]
    gate_up = jnp.dot(hidden_second, pair_full, preferred_element_type=jnp.float32)
    gate = gate_up[:, :unit_count]
    up_proj = gate_up[:, unit_count:]
    sigmoid = jax.nn.sigmoid(gate)
    activation = (gate * sigmoid * up_proj).astype(jnp.bfloat16)
    act_grad = jnp.dot(cot_low, wd_turned, preferred_element_type=jnp.float32)
    gate_grad = (act_grad * up_proj * sigmoid * (1.0 + gate * (1.0 - sigmoid))).astype(jnp.bfloat16)
    up_grad = (act_grad * gate * sigmoid).astype(jnp.bfloat16)
    pair_grad = jnp.concatenate([gate_grad, up_grad], axis=1)
    hidden2_grad, lowered = exchange(
        "tp",
        [],
        [
            contract_last(pair_grad, pair_full).astype(jnp.bfloat16),
            contract_last(activation, wd_turned).astype(jnp.bfloat16),
        ],
        5,
    )
    block_out = middle + lowered
    norm2_part = jnp.sum(hidden2_grad * normed_second, axis=0)
    middle_grad = norm_back(hidden2_grad * norm2_gain, normed_second, inv_second) + cotangent
    (mid_low,) = exchange("tp", [middle_grad.astype(jnp.bfloat16)], [], 6)
    attended_grad = jnp.dot(mid_low, wo_turned, preferred_element_type=jnp.float32).astype(
        jnp.bfloat16
    )
    grad_out = attended_grad.reshape(block_len, local_groups, group_size, head_width)
    delta_rows = jnp.transpose(
        jnp.sum(grad_out.astype(jnp.float32) * attended.astype(jnp.float32), axis=-1), (1, 2, 0)
    )
    query_side = (queries, positions, query_start, grad_out, delta_rows, log_total, score_scale)
    query_grad, key_terms = attend_back(
        all_keys, all_values, all_pos, query_side, block_len * lax.axis_size("ctx")
    )
    (stacked_grads,) = exchange("ctx", [], [key_terms], 7)
    stacked_grads = stacked_grads.reshape(block_len, 2, local_groups, head_width)
    key_grad = stacked_grads[:, 0]
    value_grad = stacked_grads[:, 1]
    query_back = rotate_back(query_grad, cosine, sine_table)
    q_gain_part = jnp.sum(query_back * query_hat, axis=(0, 1, 2))
    query_raw_grad = (
        norm_back(query_back * q_gain, query_hat, inv_query)
        .astype(jnp.bfloat16)
        .reshape(block_len, query_width)
    )
    key_back = rotate_back(key_grad, cosine, sine_table)
    k_gain_part = jnp.sum(key_back * key_hat, axis=(0, 1))
    key_raw_grad = (
        norm_back(key_back * k_gain, key_hat, inv_key)
        .astype(jnp.bfloat16)
        .reshape(block_len, key_width)
    )
    value_low = value_grad.astype(jnp.bfloat16).reshape(block_len, key_width)
    qkv_grad = jnp.concatenate([query_raw_grad, key_raw_grad, value_low], axis=1)
    (hidden1_grad,) = exchange(
        "tp", [], [contract_last(qkv_grad, qkv_full).astype(jnp.bfloat16)], 8
    )
    norm1_part = jnp.sum(hidden1_grad * normed_first, axis=0)
    input_grad = norm_back(hidden1_grad * norm1_gain, normed_first, inv_first) + middle_grad
    gain_parts = jnp.concatenate([norm1_part, norm2_part, q_gain_part, k_gain_part])
    gain_rows = -(-gain_parts.shape[0] // 1024) * 8
    gain_block = jnp.pad(gain_parts, (0, gain_rows * 128 - gain_parts.shape[0])).reshape(
        gain_rows, 128
    )
    (tp_gains,) = exchange("tp", [gain_block], [], 9)
    gain_block = jnp.sum(tp_gains.reshape(-1, gain_rows, 128), axis=0)
    ctx_gains, qkv_wgrad, pair_wgrad, out_wgrad, down_wgrad = exchange(
        "ctx",
        [gain_block],
        [
            contract_rows(hidden_first, qkv_grad).astype(jnp.bfloat16),
            contract_rows(hidden_second, pair_grad).astype(jnp.bfloat16),
            contract_rows(mid_low, attended_flat).astype(jnp.bfloat16),
            contract_rows(cot_low, activation).astype(jnp.bfloat16),
        ],
        10,
    )
    gains = jnp.sum(ctx_gains.reshape(-1, gain_rows, 128), axis=0).reshape(-1)
    width = norm1_gain.shape[0]
    return (
        block_out,
        input_grad,
        qkv_wgrad[:, :query_width],
        qkv_wgrad[:, query_width : query_width + key_width],
        qkv_wgrad[:, query_width + key_width :],
        out_wgrad.T,
        pair_wgrad[:, :unit_count],
        pair_wgrad[:, unit_count:],
        down_wgrad.T,
        gains[:width],
        gains[width : 2 * width],
        gains[2 * width : 2 * width + head_width],
        gains[2 * width + head_width : 2 * width + 2 * head_width],
    )


def solution(mesh):
    in_specs = (
        P(("ctx", "tp"), None),
        P("ctx"),
        P("ctx", "tp"),
        P("ctx", "tp"),
        P("ctx", "tp"),
        P("tp", "ctx"),
        P("ctx", "tp"),
        P("ctx", "tp"),
        P("tp", "ctx"),
        P(),
        P(),
        P(),
        P(),
        P(("ctx", "tp"), None),
    )
    out_specs = (
        P(("ctx", "tp"), None),
        P(("ctx", "tp"), None),
        P("ctx", "tp"),
        P("ctx", "tp"),
        P("ctx", "tp"),
        P("tp", "ctx"),
        P("ctx", "tp"),
        P("ctx", "tp"),
        P("tp", "ctx"),
        P(),
        P(),
        P(),
        P(),
    )
    return jax.shard_map(local, mesh=mesh, in_specs=in_specs, out_specs=out_specs, check_vma=False)
```

```python
import functools

import jax
import jax.numpy as jnp
from jax import lax
from jax.experimental import pallas as pl
from jax.experimental.pallas import tpu as pltpu
from jax.sharding import PartitionSpec as P

DOCS = 2


EPSILON = 1e-06
ROPE_BASE = 1000000.0
MASKED = -1e30
MESH = pl.DeviceIdType.MESH


def inv_rms(values):
    return lax.rsqrt(jnp.mean(values * values, axis=-1, keepdims=True) + EPSILON)


def rope_tables(positions, width):
    half_width = width // 2
    inverse = ROPE_BASE ** (-(jnp.arange(half_width, dtype=jnp.float32) * 2.0) / width)
    angles = positions.astype(jnp.float32)[:, None] * inverse[None, :]
    return (jnp.cos(angles), jnp.sin(angles))


def spread_table(table, values):
    half_width = values.shape[-1] // 2
    table_shape = (table.shape[0],) + (1,) * (values.ndim - 2) + (half_width,)
    return table.reshape(table_shape)


def rotate(values, cosine, sine_table):
    half_width = values.shape[-1] // 2
    cosine = spread_table(cosine, values)
    sine_table = spread_table(sine_table, values)
    former = values[..., :half_width]
    latter = values[..., half_width:]
    return jnp.concatenate(
        [former * cosine - latter * sine_table, latter * cosine + former * sine_table], axis=-1
    )


def rotate_back(grads, cosine, sine_table):
    half_width = grads.shape[-1] // 2
    cosine = spread_table(cosine, grads)
    sine_table = spread_table(sine_table, grads)
    former = grads[..., :half_width]
    latter = grads[..., half_width:]
    return jnp.concatenate(
        [former * cosine + latter * sine_table, latter * cosine - former * sine_table], axis=-1
    )


def norm_back(upstream, normed, inverse):
    return inverse * (upstream - normed * jnp.mean(upstream * normed, axis=-1, keepdims=True))


def contract_last(operand_left, operand_right):
    return lax.dot_general(
        operand_left, operand_right, (((1,), (1,)), ((), ())), preferred_element_type=jnp.float32
    )


def contract_rows(operand_left, operand_right):
    return lax.dot_general(
        operand_left, operand_right, (((0,), (0,)), ((), ())), preferred_element_type=jnp.float32
    )


class Line:
    def __init__(self, axis, n):
        self.axis, self.half = axis, n // 2
        self.me = lax.axis_index(axis)
        self.parity = lax.rem(self.me, 2)
        self.group = self.me // 2
        self.pair = self.me + 1 - 2 * self.parity

    def peer(self, shift):
        return lax.rem(self.group + shift, self.half) * 2 + self.parity


def exchange_kernel(gather_axes, scatter_axes, sizes, *refs):
    gather_count, scatter_count = len(gather_axes), len(scatter_axes)
    position = 0

    def take(count):
        nonlocal position
        taken = refs[position : position + count]
        position += count
        return taken

    shards, parts = take(gather_count), take(scatter_count)
    wholes, totals = take(gather_count), take(scatter_count)
    from_pair, from_peer = take(scatter_count), take(scatter_count)
    gather_sems = take(5) if gather_count else None
    scatter_sems = take(4) if scatter_count else None
    lines = {axis: Line(axis, n) for axis, n in sizes.items()}

    barrier = pltpu.get_barrier_semaphore()
    for axis, line in lines.items():
        for other in [line.pair] + [line.peer(shift) for shift in range(1, line.half)]:
            pl.semaphore_signal(barrier, inc=1, device_id={axis: other}, device_id_type=MESH)
    pl.semaphore_wait(barrier, sum(line.half for line in lines.values()))

    def push(source, target, send, receive, axis, other):
        return pltpu.make_async_remote_copy(
            src_ref=source,
            dst_ref=target,
            send_sem=send,
            recv_sem=receive,
            device_id={axis: other},
            device_id_type=MESH,
        )

    pending = []
    first = {}
    for index in range(scatter_count):
        line = lines[scatter_axes[index]]
        half, group, parity = line.half, line.group, line.parity
        send_pair, recv_pair, send_peer, recv_peer = scatter_sems
        for shift in list(range(1, half)) + [0]:
            wanted = lax.rem(group + shift, half) * 2 + 1 - parity
            first[index, shift] = push(
                parts[index].at[wanted],
                from_pair[index].at[shift],
                send_pair.at[index, shift],
                recv_pair.at[index, shift],
                line.axis,
                line.pair,
            )
            first[index, shift].start()
    direct = {}
    for index in range(gather_count):
        line = lines[gather_axes[index]]
        half, group, parity, me = line.half, line.group, line.parity, line.me
        own_sem, send_peer_g, recv_peer_g, send_pair_g, recv_pair_g = gather_sems
        own = pltpu.make_async_copy(shards[index], wholes[index].at[me], own_sem.at[index])
        own.start()
        pending.append(own.wait)
        for shift in range(1, half):
            direct[index, shift] = push(
                shards[index],
                wholes[index].at[me],
                send_peer_g.at[index, shift],
                recv_peer_g.at[index, shift],
                line.axis,
                line.peer(shift),
            )
            direct[index, shift].start()
        across = push(
            shards[index],
            wholes[index].at[me],
            send_pair_g.at[index, 0],
            recv_pair_g.at[index, 0],
            line.axis,
            line.pair,
        )
        across.start()
        pending.append(across.wait)
    second = {}
    for index in range(scatter_count):
        line = lines[scatter_axes[index]]
        half, group, parity = line.half, line.group, line.parity
        rows = parts[index].shape[1]
        chunk = min(rows, 32)
        for shift in list(range(1, half)) + [0]:
            first[index, shift].wait_recv()
            kept = line.peer(shift)

            def add_pair(step, unused, index=index, shift=shift, kept=kept, chunk=chunk):
                span = pl.ds(pl.multiple_of(step * chunk, chunk), chunk)
                summed = parts[index][kept, span, :].astype(jnp.float32) + from_pair[index][
                    shift, span, :
                ].astype(jnp.float32)
                if shift:
                    from_pair[index][shift, span, :] = summed.astype(jnp.bfloat16)
                else:
                    totals[index][span, :] = summed
                return unused

            lax.fori_loop(0, rows // chunk, add_pair, 0)
            if shift:
                second[index, shift] = push(
                    from_pair[index].at[shift],
                    from_peer[index].at[shift - 1],
                    send_peer.at[index, shift],
                    recv_peer.at[index, shift],
                    line.axis,
                    line.peer(shift),
                )
                second[index, shift].start()
    for index in range(gather_count):
        line = lines[gather_axes[index]]
        half, group, parity, me = line.half, line.group, line.parity, line.me
        for shift in range(1, half):
            direct[index, shift].wait_recv()
            origin = lax.rem(group + half - shift, half) * 2 + parity
            onward = push(
                wholes[index].at[origin],
                wholes[index].at[origin],
                send_pair_g.at[index, shift],
                recv_pair_g.at[index, shift],
                line.axis,
                line.pair,
            )
            onward.start()
            pending.append(direct[index, shift].wait_send)
            pending.append(onward.wait)
    for index in range(scatter_count):
        line = lines[scatter_axes[index]]
        half, group, parity = line.half, line.group, line.parity
        rows = parts[index].shape[1]
        chunk = min(rows, 32)
        for shift in range(1, half):
            second[index, shift].wait_recv()

        def add_peers(step, unused, index=index, chunk=chunk, half=half):
            span = pl.ds(pl.multiple_of(step * chunk, chunk), chunk)
            summed = totals[index][span, :]
            for shift in range(1, half):
                summed += from_peer[index][shift - 1, span, :].astype(jnp.float32)
            totals[index][span, :] = summed
            return unused

        lax.fori_loop(0, rows // chunk, add_peers, 0)
        for shift in range(half):
            pending.append(first[index, shift].wait_send)
            if shift:
                pending.append(second[index, shift].wait_send)
    for wait in pending:
        wait()


def exchange(gathers, scatters, number):
    axes = sorted({axis for axis, unused in gathers + scatters})
    sizes = {axis: lax.axis_size(axis) for axis in axes}
    most = max(sizes.values()) // 2
    shards = [shard for unused, shard in gathers]
    split = [
        part.reshape((sizes[axis], part.shape[0] // sizes[axis]) + part.shape[1:])
        for axis, part in scatters
    ]
    anywhere = pl.BlockSpec(memory_space=pl.ANY)
    vmem = pl.BlockSpec(memory_space=pltpu.VMEM)
    dma = pltpu.SemaphoreType.DMA
    scratch = [pltpu.VMEM((part.shape[0] // 2,) + part.shape[1:], part.dtype) for part in split]
    scratch += [
        pltpu.VMEM((part.shape[0] // 2 - 1,) + part.shape[1:], part.dtype) for part in split
    ]
    if gathers:
        scratch += [dma((len(gathers),))] + [dma((len(gathers), most))] * 4
    if scatters:
        scratch += [dma((len(scatters), most))] * 4
    wholes = [
        jax.ShapeDtypeStruct((sizes[axis],) + shard.shape, shard.dtype) for axis, shard in gathers
    ]
    results = pl.pallas_call(
        functools.partial(
            exchange_kernel,
            tuple(axis for axis, unused in gathers),
            tuple(axis for axis, unused in scatters),
            sizes,
        ),
        out_shape=wholes + [jax.ShapeDtypeStruct(part.shape[1:], jnp.float32) for part in split],
        in_specs=[anywhere] * len(gathers) + [vmem] * len(split),
        out_specs=[anywhere] * len(gathers) + [vmem] * len(split),
        scratch_shapes=scratch,
        compiler_params=pltpu.CompilerParams(
            collective_id=number,
            has_side_effects=True,
            vmem_limit_bytes=(48 if scatters else 4) * 1024 * 1024,
        ),
    )(*shards, *split)
    return [
        whole.reshape((-1,) + shard.shape[1:]) for whole, shard in zip(results, shards)
    ] + list(results[len(shards) :])


def turned(operand_left, operand_right):
    return lax.dot_general(
        operand_left, operand_right, (((0,), (0,)), ((), ())), preferred_element_type=jnp.float32
    )


def needed(blocks_ref, own_ref, index, doc_blocks):
    block, own = blocks_ref[index], own_ref[0]
    return jnp.logical_and(block <= own, block >= own - lax.rem(own, doc_blocks))


def attend_kernel(
    scale, heads, groups, doc_blocks, blocks_ref, own_ref, q_ref, k_ref, v_ref, out_ref, log_ref,
    top_ref, total_ref, mixed_ref,
):
    length = q_ref.shape[0]
    width = q_ref.shape[1] // heads
    top_ref[...] = jnp.full_like(top_ref, MASKED)
    total_ref[...] = jnp.zeros_like(total_ref)
    mixed_ref[...] = jnp.zeros_like(mixed_ref)

    def visit(index, unused):
        @pl.when(needed(blocks_ref, own_ref, index, doc_blocks))
        def attend_work():
            ahead = (own_ref[0] - blocks_ref[index]) * length
            rows = pl.ds(pl.multiple_of(index * length, length), length)
            allowed = lax.broadcasted_iota(jnp.int32, (length, length), 1) <= (
                lax.broadcasted_iota(jnp.int32, (length, length), 0) + ahead
            )
            for head in range(heads):
                group = head * groups // heads
                columns = pl.ds(head * width, width)
                shared = pl.ds(group * width, width)
                scores = contract_last(q_ref[:, columns], k_ref[rows, shared]) * scale
                scores = jnp.where(allowed, scores, MASKED)
                old_top = top_ref[head]
                new_top = jnp.maximum(old_top, jnp.max(scores, axis=1, keepdims=True))
                probs = jnp.exp(scores - new_top)
                factor = jnp.exp(old_top - new_top)
                top_ref[head] = new_top
                total_ref[head] = total_ref[head] * factor + jnp.sum(probs, axis=1, keepdims=True)
                mixed_ref[:, columns] = mixed_ref[:, columns] * factor + jnp.dot(
                    probs.astype(jnp.bfloat16), v_ref[rows, shared],
                    preferred_element_type=jnp.float32,
                )

        return unused

    lax.fori_loop(0, k_ref.shape[0] // length, visit, 0)
    for head in range(heads):
        columns = pl.ds(head * width, width)
        out_ref[:, columns] = (mixed_ref[:, columns] / total_ref[head]).astype(out_ref.dtype)
        log_ref[head] = top_ref[head] + jnp.log(total_ref[head])


def attend_back_kernel(
    scale, heads, groups, doc_blocks, blocks_ref, own_ref, q_ref, k_ref, v_ref, grad_ref, log_ref,
    delta_ref, query_ref, terms_ref,
):
    length = q_ref.shape[0]
    width = q_ref.shape[1] // heads
    query_ref[...] = jnp.zeros_like(query_ref)

    def visit(index, unused):
        rows = pl.ds(pl.multiple_of(index * length, length), length)
        used = needed(blocks_ref, own_ref, index, doc_blocks)

        @pl.when(jnp.logical_not(used))
        def skipped():
            terms_ref[rows, :] = jnp.zeros((length, terms_ref.shape[1]), terms_ref.dtype)

        @pl.when(used)
        def grad_work():
            ahead = (own_ref[0] - blocks_ref[index]) * length
            allowed = lax.broadcasted_iota(jnp.int32, (length, length), 0) <= (
                lax.broadcasted_iota(jnp.int32, (length, length), 1) + ahead
            )
            for group in range(groups):
                shared = pl.ds(group * width, width)
                keys_part, values_part = k_ref[rows, shared], v_ref[rows, shared]
                key_sum = value_sum = None
                for head in range(group * heads // groups, (group + 1) * heads // groups):
                    columns = pl.ds(head * width, width)
                    queries, grad_out = q_ref[:, columns], grad_ref[:, columns]
                    scores = contract_last(keys_part, queries) * scale
                    probs = jnp.where(allowed, jnp.exp(scores - log_ref[head]), 0.0)
                    prob_grad = contract_last(values_part, grad_out)
                    score_low = (probs * (prob_grad - delta_ref[head])).astype(jnp.bfloat16)
                    value_part = jnp.dot(
                        probs.astype(jnp.bfloat16), grad_out, preferred_element_type=jnp.float32
                    )
                    key_part = jnp.dot(score_low, queries, preferred_element_type=jnp.float32)
                    key_sum = key_part if key_sum is None else key_sum + key_part
                    value_sum = value_part if value_sum is None else value_sum + value_part
                    query_ref[:, columns] += turned(score_low, keys_part)
                terms_ref[rows, shared] = (key_sum * scale).astype(terms_ref.dtype)
                terms_ref[rows, pl.ds((groups + group) * width, width)] = value_sum.astype(
                    terms_ref.dtype
                )

        return unused

    lax.fori_loop(0, k_ref.shape[0] // length, visit, 0)
    query_ref[...] = query_ref[...] * scale


def attention_call(kernel, settings, inputs, outputs, scratch):
    smem = pl.BlockSpec(memory_space=pltpu.SMEM)
    vmem = pl.BlockSpec(memory_space=pltpu.VMEM)
    return pl.pallas_call(
        functools.partial(kernel, *settings),
        out_shape=outputs,
        in_specs=[smem, smem] + [vmem] * (len(inputs) - 2),
        out_specs=[vmem] * len(outputs),
        scratch_shapes=scratch,
        compiler_params=pltpu.CompilerParams(vmem_limit_bytes=56 * 1024 * 1024),
    )(*inputs)


def local(
    tokens,
    positions,
    q_weight,
    k_weight,
    v_weight,
    o_weight,
    gate_weight,
    up_weight,
    down_weight,
    norm1_gain,
    norm2_gain,
    q_gain,
    k_gain,
    cotangent,
):
    head_width = q_gain.shape[0]
    score_scale = head_width ** (-0.5)
    local_heads = q_weight.shape[1] // head_width
    local_groups = k_weight.shape[1] // head_width
    group_size = local_heads // local_groups
    doc_len = positions.shape[0] * lax.axis_size("ctx") // DOCS
    qkv_shard = jnp.concatenate([q_weight, k_weight, v_weight], axis=1)
    pair_shard = jnp.concatenate([gate_weight, up_weight], axis=1)
    inv_first = inv_rms(tokens)
    normed_first = tokens * inv_first
    qkv_full, hidden_first, cot_low, wo_turned, pair_full, wd_turned, all_pos = exchange(
        [
            ("ctx", qkv_shard),
            ("tp", (normed_first * norm1_gain).astype(jnp.bfloat16)),
            ("tp", cotangent.astype(jnp.bfloat16)),
            ("ctx", o_weight.T),
            ("ctx", pair_shard),
            ("ctx", down_weight.T),
            ("ctx", positions.reshape(-1, 128)),
        ],
        [],
        0,
    )
    block_len = hidden_first.shape[0]
    key_blocks = all_pos.reshape(-1, block_len)[:, 0] // block_len
    own_block = positions[:1] // block_len
    local_pos = positions % doc_len
    query_start = positions - local_pos
    cosine, sine_table = rope_tables(local_pos, head_width)
    query_width = local_heads * head_width
    key_width = local_groups * head_width
    raw = jnp.dot(hidden_first, qkv_full, preferred_element_type=jnp.float32)
    query_raw = raw[:, :query_width].reshape(block_len, local_groups, group_size, head_width)
    key_raw = raw[:, query_width : query_width + key_width].reshape(
        block_len, local_groups, head_width
    )
    values_local = raw[:, query_width + key_width :].astype(jnp.bfloat16)
    inv_query = inv_rms(query_raw)
    query_hat = query_raw * inv_query
    queries = rotate(query_hat * q_gain, cosine, sine_table).astype(jnp.bfloat16)
    inv_key = inv_rms(key_raw)
    key_hat = key_raw * inv_key
    keys_local = rotate(key_hat * k_gain, cosine, sine_table).astype(jnp.bfloat16)
    queries = queries.reshape(block_len, query_width)
    all_keys, all_values = exchange(
        [("ctx", keys_local.reshape(block_len, key_width)), ("ctx", values_local)], [], 2
    )
    settings = (score_scale, local_heads, local_groups, doc_len // block_len)
    attended_flat, log_total = attention_call(
        attend_kernel,
        settings,
        (key_blocks, own_block, queries, all_keys, all_values),
        [
            jax.ShapeDtypeStruct((block_len, query_width), jnp.bfloat16),
            jax.ShapeDtypeStruct((local_heads, block_len, 1), jnp.float32),
        ],
        [
            pltpu.VMEM((local_heads, block_len, 1), jnp.float32),
            pltpu.VMEM((local_heads, block_len, 1), jnp.float32),
            pltpu.VMEM((block_len, query_width), jnp.float32),
        ],
    )
    (projected,) = exchange(
        [], [("tp", contract_last(attended_flat, wo_turned).astype(jnp.bfloat16))], 3
    )
    middle = tokens + projected
    inv_second = inv_rms(middle)
    normed_second = middle * inv_second
    (hidden_second,) = exchange(
        [("tp", (normed_second * norm2_gain).astype(jnp.bfloat16))], [], 4
    )
    unit_count = gate_weight.shape[1]
    gate_up = jnp.dot(hidden_second, pair_full, preferred_element_type=jnp.float32)
    gate = gate_up[:, :unit_count]
    up_proj = gate_up[:, unit_count:]
    sigmoid = jax.nn.sigmoid(gate)
    activation = (gate * sigmoid * up_proj).astype(jnp.bfloat16)
    act_grad = jnp.dot(cot_low, wd_turned, preferred_element_type=jnp.float32)
    gate_grad = (act_grad * up_proj * sigmoid * (1.0 + gate * (1.0 - sigmoid))).astype(jnp.bfloat16)
    up_grad = (act_grad * gate * sigmoid).astype(jnp.bfloat16)
    pair_grad = jnp.concatenate([gate_grad, up_grad], axis=1)
    hidden2_grad, lowered = exchange(
        [],
        [
            ("tp", contract_last(pair_grad, pair_full).astype(jnp.bfloat16)),
            ("tp", contract_last(activation, wd_turned).astype(jnp.bfloat16)),
        ],
        5,
    )
    block_out = middle + lowered
    norm2_part = jnp.sum(hidden2_grad * normed_second, axis=0)
    middle_grad = norm_back(hidden2_grad * norm2_gain, normed_second, inv_second) + cotangent
    (mid_low,) = exchange([("tp", middle_grad.astype(jnp.bfloat16))], [], 6)
    attended_grad = jnp.dot(mid_low, wo_turned, preferred_element_type=jnp.float32).astype(
        jnp.bfloat16
    )
    delta_rows = jnp.sum(
        (attended_grad.astype(jnp.float32) * attended_flat.astype(jnp.float32)).reshape(
            block_len, local_heads, head_width
        ),
        axis=-1,
    )
    query_grad, key_terms = attention_call(
        attend_back_kernel,
        settings,
        (
            key_blocks,
            own_block,
            queries,
            all_keys,
            all_values,
            attended_grad,
            log_total.reshape(local_heads, 1, block_len),
            delta_rows.T.reshape(local_heads, 1, block_len),
        ),
        [
            jax.ShapeDtypeStruct((block_len, query_width), jnp.float32),
            jax.ShapeDtypeStruct((all_keys.shape[0], 2 * key_width), jnp.bfloat16),
        ],
        [],
    )
    query_grad = query_grad.reshape(block_len, local_groups, group_size, head_width)
    (stacked_grads,) = exchange([], [("ctx", key_terms)], 7)
    stacked_grads = stacked_grads.reshape(block_len, 2, local_groups, head_width)
    key_grad = stacked_grads[:, 0]
    value_grad = stacked_grads[:, 1]
    query_back = rotate_back(query_grad, cosine, sine_table)
    q_gain_part = jnp.sum(query_back * query_hat, axis=(0, 1, 2))
    query_raw_grad = (
        norm_back(query_back * q_gain, query_hat, inv_query)
        .astype(jnp.bfloat16)
        .reshape(block_len, query_width)
    )
    key_back = rotate_back(key_grad, cosine, sine_table)
    k_gain_part = jnp.sum(key_back * key_hat, axis=(0, 1))
    key_raw_grad = (
        norm_back(key_back * k_gain, key_hat, inv_key)
        .astype(jnp.bfloat16)
        .reshape(block_len, key_width)
    )
    value_low = value_grad.astype(jnp.bfloat16).reshape(block_len, key_width)
    qkv_grad = jnp.concatenate([query_raw_grad, key_raw_grad, value_low], axis=1)
    (hidden1_grad,) = exchange(
        [], [("tp", contract_last(qkv_grad, qkv_full).astype(jnp.bfloat16))], 8
    )
    norm1_part = jnp.sum(hidden1_grad * normed_first, axis=0)
    input_grad = norm_back(hidden1_grad * norm1_gain, normed_first, inv_first) + middle_grad
    gain_parts = jnp.concatenate([norm1_part, norm2_part, q_gain_part, k_gain_part])
    gain_rows = -(-gain_parts.shape[0] // 1024) * 8
    gain_block = jnp.pad(gain_parts, (0, gain_rows * 128 - gain_parts.shape[0])).reshape(
        gain_rows, 128
    )
    (tp_gains,) = exchange([("tp", gain_block)], [], 9)
    gain_block = jnp.sum(tp_gains.reshape(-1, gain_rows, 128), axis=0)
    ctx_gains, qkv_wgrad, pair_wgrad, out_wgrad, down_wgrad = exchange(
        [("ctx", gain_block)],
        [
            ("ctx", contract_rows(hidden_first, qkv_grad).astype(jnp.bfloat16)),
            ("ctx", contract_rows(hidden_second, pair_grad).astype(jnp.bfloat16)),
            ("ctx", contract_rows(mid_low, attended_flat).astype(jnp.bfloat16)),
            ("ctx", contract_rows(cot_low, activation).astype(jnp.bfloat16)),
        ],
        10,
    )
    gains = jnp.sum(ctx_gains.reshape(-1, gain_rows, 128), axis=0).reshape(-1)
    width = norm1_gain.shape[0]
    return (
        block_out,
        input_grad,
        qkv_wgrad[:, :query_width],
        qkv_wgrad[:, query_width : query_width + key_width],
        qkv_wgrad[:, query_width + key_width :],
        out_wgrad.T,
        pair_wgrad[:, :unit_count],
        pair_wgrad[:, unit_count:],
        down_wgrad.T,
        gains[:width],
        gains[width : 2 * width],
        gains[2 * width : 2 * width + head_width],
        gains[2 * width + head_width : 2 * width + 2 * head_width],
    )


def solution(mesh):
    in_specs = (
        P(("ctx", "tp"), None),
        P("ctx"),
        P("ctx", "tp"),
        P("ctx", "tp"),
        P("ctx", "tp"),
        P("tp", "ctx"),
        P("ctx", "tp"),
        P("ctx", "tp"),
        P("tp", "ctx"),
        P(),
        P(),
        P(),
        P(),
        P(("ctx", "tp"), None),
    )
    out_specs = (
        P(("ctx", "tp"), None),
        P(("ctx", "tp"), None),
        P("ctx", "tp"),
        P("ctx", "tp"),
        P("ctx", "tp"),
        P("tp", "ctx"),
        P("ctx", "tp"),
        P("ctx", "tp"),
        P("tp", "ctx"),
        P(),
        P(),
        P(),
        P(),
    )
    return jax.shard_map(local, mesh=mesh, in_specs=in_specs, out_specs=out_specs, check_vma=False)
```

```python
import functools

import jax
import jax.numpy as jnp
from jax import lax
from jax.experimental import pallas as pl
from jax.experimental.pallas import tpu as pltpu
from jax.sharding import PartitionSpec as P

DOCS = 2


EPSILON = 1e-06
ROPE_BASE = 1000000.0
MASKED = -1e30
MESH = pl.DeviceIdType.MESH


def inv_rms(values):
    return lax.rsqrt(jnp.mean(values * values, axis=-1, keepdims=True) + EPSILON)


def rope_tables(positions, width):
    half_width = width // 2
    inverse = ROPE_BASE ** (-(jnp.arange(half_width, dtype=jnp.float32) * 2.0) / width)
    angles = positions.astype(jnp.float32)[:, None] * inverse[None, :]
    return (jnp.cos(angles), jnp.sin(angles))


def by_head(flat, width):
    return jnp.stack([flat[:, at : at + width] for at in range(0, flat.shape[1], width)])


def by_row(heads):
    return jnp.concatenate([heads[head] for head in range(heads.shape[0])], axis=1)


def rotate(values, cosine, sine_table):
    half_width = values.shape[-1] // 2
    former = values[..., :half_width]
    latter = values[..., half_width:]
    return jnp.concatenate(
        [former * cosine - latter * sine_table, latter * cosine + former * sine_table], axis=-1
    )


def rotate_back(grads, cosine, sine_table):
    half_width = grads.shape[-1] // 2
    former = grads[..., :half_width]
    latter = grads[..., half_width:]
    return jnp.concatenate(
        [former * cosine + latter * sine_table, latter * cosine - former * sine_table], axis=-1
    )


def norm_back(upstream, normed, inverse):
    return inverse * (upstream - normed * jnp.mean(upstream * normed, axis=-1, keepdims=True))


def contract_last(operand_left, operand_right):
    return lax.dot_general(
        operand_left, operand_right, (((1,), (1,)), ((), ())), preferred_element_type=jnp.float32
    )


def contract_rows(operand_left, operand_right):
    return lax.dot_general(
        operand_left, operand_right, (((0,), (0,)), ((), ())), preferred_element_type=jnp.float32
    )


class Line:
    def __init__(self, axis, n):
        self.axis, self.half = axis, n // 2
        self.me = lax.axis_index(axis)
        self.parity = lax.rem(self.me, 2)
        self.group = self.me // 2
        self.pair = self.me + 1 - 2 * self.parity

    def peer(self, shift):
        return lax.rem(self.group + shift, self.half) * 2 + self.parity


def exchange_kernel(gather_axes, scatter_axes, sizes, *refs):
    gather_count, scatter_count = len(gather_axes), len(scatter_axes)
    position = 0

    def take(count):
        nonlocal position
        taken = refs[position : position + count]
        position += count
        return taken

    shards, parts = take(gather_count), take(scatter_count)
    wholes, totals = take(gather_count), take(scatter_count)
    from_pair, from_peer = take(scatter_count), take(scatter_count)
    gather_sems = take(5) if gather_count else None
    scatter_sems = take(4) if scatter_count else None
    lines = {axis: Line(axis, n) for axis, n in sizes.items()}

    barrier = pltpu.get_barrier_semaphore()
    for axis, line in lines.items():
        for other in [line.pair] + [line.peer(shift) for shift in range(1, line.half)]:
            pl.semaphore_signal(barrier, inc=1, device_id={axis: other}, device_id_type=MESH)
    pl.semaphore_wait(barrier, sum(line.half for line in lines.values()))

    def push(source, target, send, receive, axis, other):
        return pltpu.make_async_remote_copy(
            src_ref=source,
            dst_ref=target,
            send_sem=send,
            recv_sem=receive,
            device_id={axis: other},
            device_id_type=MESH,
        )

    pending = []
    first = {}
    for index in range(scatter_count):
        line = lines[scatter_axes[index]]
        half, group, parity = line.half, line.group, line.parity
        send_pair, recv_pair, send_peer, recv_peer = scatter_sems
        for shift in list(range(1, half)) + [0]:
            wanted = lax.rem(group + shift, half) * 2 + 1 - parity
            first[index, shift] = push(
                parts[index].at[wanted],
                from_pair[index].at[shift],
                send_pair.at[index, shift],
                recv_pair.at[index, shift],
                line.axis,
                line.pair,
            )
            first[index, shift].start()
    direct = {}
    for index in range(gather_count):
        line = lines[gather_axes[index]]
        half, group, parity, me = line.half, line.group, line.parity, line.me
        own_sem, send_peer_g, recv_peer_g, send_pair_g, recv_pair_g = gather_sems
        own = pltpu.make_async_copy(shards[index], wholes[index].at[me], own_sem.at[index])
        own.start()
        pending.append(own.wait)
        for shift in range(1, half):
            direct[index, shift] = push(
                shards[index],
                wholes[index].at[me],
                send_peer_g.at[index, shift],
                recv_peer_g.at[index, shift],
                line.axis,
                line.peer(shift),
            )
            direct[index, shift].start()
        across = push(
            shards[index],
            wholes[index].at[me],
            send_pair_g.at[index, 0],
            recv_pair_g.at[index, 0],
            line.axis,
            line.pair,
        )
        across.start()
        pending.append(across.wait)
    second = {}
    for index in range(scatter_count):
        line = lines[scatter_axes[index]]
        half, group, parity = line.half, line.group, line.parity
        rows = parts[index].shape[1]
        chunk = min(rows, 32)
        for shift in list(range(1, half)) + [0]:
            first[index, shift].wait_recv()
            kept = line.peer(shift)

            def add_pair(step, unused, index=index, shift=shift, kept=kept, chunk=chunk):
                span = pl.ds(pl.multiple_of(step * chunk, chunk), chunk)
                summed = parts[index][kept, span, :].astype(jnp.float32) + from_pair[index][
                    shift, span, :
                ].astype(jnp.float32)
                if shift:
                    from_pair[index][shift, span, :] = summed.astype(jnp.bfloat16)
                else:
                    totals[index][span, :] = summed
                return unused

            lax.fori_loop(0, rows // chunk, add_pair, 0)
            if shift:
                second[index, shift] = push(
                    from_pair[index].at[shift],
                    from_peer[index].at[shift - 1],
                    send_peer.at[index, shift],
                    recv_peer.at[index, shift],
                    line.axis,
                    line.peer(shift),
                )
                second[index, shift].start()
    for index in range(gather_count):
        line = lines[gather_axes[index]]
        half, group, parity, me = line.half, line.group, line.parity, line.me
        for shift in range(1, half):
            direct[index, shift].wait_recv()
            origin = lax.rem(group + half - shift, half) * 2 + parity
            onward = push(
                wholes[index].at[origin],
                wholes[index].at[origin],
                send_pair_g.at[index, shift],
                recv_pair_g.at[index, shift],
                line.axis,
                line.pair,
            )
            onward.start()
            pending.append(direct[index, shift].wait_send)
            pending.append(onward.wait)
    for index in range(scatter_count):
        line = lines[scatter_axes[index]]
        half, group, parity = line.half, line.group, line.parity
        rows = parts[index].shape[1]
        chunk = min(rows, 32)
        for shift in range(1, half):
            second[index, shift].wait_recv()

        def add_peers(step, unused, index=index, chunk=chunk, half=half):
            span = pl.ds(pl.multiple_of(step * chunk, chunk), chunk)
            summed = totals[index][span, :]
            for shift in range(1, half):
                summed += from_peer[index][shift - 1, span, :].astype(jnp.float32)
            totals[index][span, :] = summed
            return unused

        lax.fori_loop(0, rows // chunk, add_peers, 0)
        for shift in range(half):
            pending.append(first[index, shift].wait_send)
            if shift:
                pending.append(second[index, shift].wait_send)
    for wait in pending:
        wait()


def exchange(gathers, scatters, number):
    axes = sorted({axis for axis, unused in gathers + scatters})
    sizes = {axis: lax.axis_size(axis) for axis in axes}
    most = max(sizes.values()) // 2
    shards = [shard for unused, shard in gathers]
    split = [
        part.reshape((sizes[axis], part.shape[0] // sizes[axis]) + part.shape[1:])
        for axis, part in scatters
    ]
    anywhere = pl.BlockSpec(memory_space=pl.ANY)
    vmem = pl.BlockSpec(memory_space=pltpu.VMEM)
    dma = pltpu.SemaphoreType.DMA
    scratch = [pltpu.VMEM((part.shape[0] // 2,) + part.shape[1:], part.dtype) for part in split]
    scratch += [
        pltpu.VMEM((part.shape[0] // 2 - 1,) + part.shape[1:], part.dtype) for part in split
    ]
    if gathers:
        scratch += [dma((len(gathers),))] + [dma((len(gathers), most))] * 4
    if scatters:
        scratch += [dma((len(scatters), most))] * 4
    wholes = [
        jax.ShapeDtypeStruct((sizes[axis],) + shard.shape, shard.dtype) for axis, shard in gathers
    ]
    results = pl.pallas_call(
        functools.partial(
            exchange_kernel,
            tuple(axis for axis, unused in gathers),
            tuple(axis for axis, unused in scatters),
            sizes,
        ),
        out_shape=wholes + [jax.ShapeDtypeStruct(part.shape[1:], jnp.float32) for part in split],
        in_specs=[anywhere] * len(gathers) + [vmem] * len(split),
        out_specs=[anywhere] * len(gathers) + [vmem] * len(split),
        scratch_shapes=scratch,
        compiler_params=pltpu.CompilerParams(
            collective_id=number,
            has_side_effects=True,
            vmem_limit_bytes=(48 if scatters else 4) * 1024 * 1024,
        ),
    )(*shards, *split)
    return [
        whole.reshape((-1,) + shard.shape[1:]) for whole, shard in zip(results, shards)
    ] + list(results[len(shards) :])


def turned(operand_left, operand_right):
    return lax.dot_general(
        operand_left, operand_right, (((0,), (0,)), ((), ())), preferred_element_type=jnp.float32
    )


def needed(blocks_ref, own_ref, index, doc_blocks):
    block, own = blocks_ref[index], own_ref[0]
    return jnp.logical_and(block <= own, block >= own - lax.rem(own, doc_blocks))


def attend_kernel(
    scale, heads, groups, doc_blocks, blocks_ref, own_ref, q_ref, k_ref, v_ref, out_ref, log_ref,
    top_ref, total_ref, mixed_ref,
):
    length = q_ref.shape[0]
    width = q_ref.shape[1] // heads
    top_ref[...] = jnp.full_like(top_ref, MASKED)
    total_ref[...] = jnp.zeros_like(total_ref)
    mixed_ref[...] = jnp.zeros_like(mixed_ref)

    def visit(index, unused):
        @pl.when(needed(blocks_ref, own_ref, index, doc_blocks))
        def attend_work():
            ahead = (own_ref[0] - blocks_ref[index]) * length
            rows = pl.ds(pl.multiple_of(index * length, length), length)
            allowed = lax.broadcasted_iota(jnp.int32, (length, length), 1) <= (
                lax.broadcasted_iota(jnp.int32, (length, length), 0) + ahead
            )
            for head in range(heads):
                group = head * groups // heads
                columns = pl.ds(head * width, width)
                shared = pl.ds(group * width, width)
                scores = contract_last(q_ref[:, columns], k_ref[rows, shared]) * scale
                scores = jnp.where(allowed, scores, MASKED)
                old_top = top_ref[head]
                new_top = jnp.maximum(old_top, jnp.max(scores, axis=1, keepdims=True))
                probs = jnp.exp(scores - new_top)
                factor = jnp.exp(old_top - new_top)
                top_ref[head] = new_top
                total_ref[head] = total_ref[head] * factor + jnp.sum(probs, axis=1, keepdims=True)
                mixed_ref[:, columns] = mixed_ref[:, columns] * factor + jnp.dot(
                    probs.astype(jnp.bfloat16), v_ref[rows, shared],
                    preferred_element_type=jnp.float32,
                )

        return unused

    lax.fori_loop(0, k_ref.shape[0] // length, visit, 0)
    for head in range(heads):
        columns = pl.ds(head * width, width)
        out_ref[:, columns] = (mixed_ref[:, columns] / total_ref[head]).astype(out_ref.dtype)
        log_ref[head] = top_ref[head] + jnp.log(total_ref[head])


def attend_back_kernel(
    scale, heads, groups, doc_blocks, blocks_ref, own_ref, q_ref, k_ref, v_ref, grad_ref, log_ref,
    delta_ref, query_ref, terms_ref,
):
    length = q_ref.shape[0]
    width = q_ref.shape[1] // heads
    query_ref[...] = jnp.zeros_like(query_ref)

    def visit(index, unused):
        rows = pl.ds(pl.multiple_of(index * length, length), length)
        used = needed(blocks_ref, own_ref, index, doc_blocks)

        @pl.when(jnp.logical_not(used))
        def skipped():
            terms_ref[rows, :] = jnp.zeros((length, terms_ref.shape[1]), terms_ref.dtype)

        @pl.when(used)
        def grad_work():
            ahead = (own_ref[0] - blocks_ref[index]) * length
            allowed = lax.broadcasted_iota(jnp.int32, (length, length), 0) <= (
                lax.broadcasted_iota(jnp.int32, (length, length), 1) + ahead
            )
            for group in range(groups):
                shared = pl.ds(group * width, width)
                keys_part, values_part = k_ref[rows, shared], v_ref[rows, shared]
                key_sum = value_sum = None
                for head in range(group * heads // groups, (group + 1) * heads // groups):
                    columns = pl.ds(head * width, width)
                    queries, grad_out = q_ref[:, columns], grad_ref[:, columns]
                    scores = contract_last(keys_part, queries) * scale
                    probs = jnp.where(allowed, jnp.exp(scores - log_ref[head]), 0.0)
                    prob_grad = contract_last(values_part, grad_out)
                    score_low = (probs * (prob_grad - delta_ref[head])).astype(jnp.bfloat16)
                    value_part = jnp.dot(
                        probs.astype(jnp.bfloat16), grad_out, preferred_element_type=jnp.float32
                    )
                    key_part = jnp.dot(score_low, queries, preferred_element_type=jnp.float32)
                    key_sum = key_part if key_sum is None else key_sum + key_part
                    value_sum = value_part if value_sum is None else value_sum + value_part
                    query_ref[:, columns] += turned(score_low, keys_part)
                terms_ref[rows, shared] = (key_sum * scale).astype(terms_ref.dtype)
                terms_ref[rows, pl.ds((groups + group) * width, width)] = value_sum.astype(
                    terms_ref.dtype
                )

        return unused

    lax.fori_loop(0, k_ref.shape[0] // length, visit, 0)
    query_ref[...] = query_ref[...] * scale


def attention_call(kernel, settings, inputs, outputs, scratch):
    smem = pl.BlockSpec(memory_space=pltpu.SMEM)
    vmem = pl.BlockSpec(memory_space=pltpu.VMEM)
    return pl.pallas_call(
        functools.partial(kernel, *settings),
        out_shape=outputs,
        in_specs=[smem, smem] + [vmem] * (len(inputs) - 2),
        out_specs=[vmem] * len(outputs),
        scratch_shapes=scratch,
        compiler_params=pltpu.CompilerParams(vmem_limit_bytes=56 * 1024 * 1024),
    )(*inputs)


def local(
    tokens,
    positions,
    q_weight,
    k_weight,
    v_weight,
    o_weight,
    gate_weight,
    up_weight,
    down_weight,
    norm1_gain,
    norm2_gain,
    q_gain,
    k_gain,
    cotangent,
):
    head_width = q_gain.shape[0]
    score_scale = head_width ** (-0.5)
    local_heads = q_weight.shape[1] // head_width
    local_groups = k_weight.shape[1] // head_width
    doc_len = positions.shape[0] * lax.axis_size("ctx") // DOCS
    qkv_shard = jnp.concatenate([q_weight, k_weight, v_weight], axis=1)
    pair_shard = jnp.concatenate([gate_weight, up_weight], axis=1)
    inv_first = inv_rms(tokens)
    normed_first = tokens * inv_first
    qkv_full, hidden_first, cot_low, wo_turned, pair_full, wd_turned, all_pos = exchange(
        [
            ("ctx", qkv_shard),
            ("tp", (normed_first * norm1_gain).astype(jnp.bfloat16)),
            ("tp", cotangent.astype(jnp.bfloat16)),
            ("ctx", o_weight.T),
            ("ctx", pair_shard),
            ("ctx", down_weight.T),
            ("ctx", positions.reshape(-1, 128)),
        ],
        [],
        0,
    )
    block_len = hidden_first.shape[0]
    key_blocks = all_pos.reshape(-1, block_len)[:, 0] // block_len
    own_block = positions[:1] // block_len
    local_pos = positions % doc_len
    query_start = positions - local_pos
    cosine, sine_table = rope_tables(local_pos, head_width)
    query_width = local_heads * head_width
    key_width = local_groups * head_width
    raw = jnp.dot(hidden_first, qkv_full, preferred_element_type=jnp.float32)
    query_raw = by_head(raw[:, :query_width], head_width)
    key_raw = by_head(raw[:, query_width : query_width + key_width], head_width)
    values_local = raw[:, query_width + key_width :].astype(jnp.bfloat16)
    inv_query = inv_rms(query_raw)
    query_hat = query_raw * inv_query
    queries = rotate(query_hat * q_gain, cosine, sine_table).astype(jnp.bfloat16)
    inv_key = inv_rms(key_raw)
    key_hat = key_raw * inv_key
    keys_local = rotate(key_hat * k_gain, cosine, sine_table).astype(jnp.bfloat16)
    queries = by_row(queries)
    all_keys, all_values = exchange(
        [("ctx", by_row(keys_local)), ("ctx", values_local)], [], 2
    )
    settings = (score_scale, local_heads, local_groups, doc_len // block_len)
    attended_flat, log_total = attention_call(
        attend_kernel,
        settings,
        (key_blocks, own_block, queries, all_keys, all_values),
        [
            jax.ShapeDtypeStruct((block_len, query_width), jnp.bfloat16),
            jax.ShapeDtypeStruct((local_heads, block_len, 1), jnp.float32),
        ],
        [
            pltpu.VMEM((local_heads, block_len, 1), jnp.float32),
            pltpu.VMEM((local_heads, block_len, 1), jnp.float32),
            pltpu.VMEM((block_len, query_width), jnp.float32),
        ],
    )
    (projected,) = exchange(
        [], [("tp", contract_last(attended_flat, wo_turned).astype(jnp.bfloat16))], 3
    )
    middle = tokens + projected
    inv_second = inv_rms(middle)
    normed_second = middle * inv_second
    (hidden_second,) = exchange(
        [("tp", (normed_second * norm2_gain).astype(jnp.bfloat16))], [], 4
    )
    unit_count = gate_weight.shape[1]
    gate_up = jnp.dot(hidden_second, pair_full, preferred_element_type=jnp.float32)
    gate = gate_up[:, :unit_count]
    up_proj = gate_up[:, unit_count:]
    sigmoid = jax.nn.sigmoid(gate)
    activation = (gate * sigmoid * up_proj).astype(jnp.bfloat16)
    act_grad = jnp.dot(cot_low, wd_turned, preferred_element_type=jnp.float32)
    gate_grad = (act_grad * up_proj * sigmoid * (1.0 + gate * (1.0 - sigmoid))).astype(jnp.bfloat16)
    up_grad = (act_grad * gate * sigmoid).astype(jnp.bfloat16)
    pair_grad = jnp.concatenate([gate_grad, up_grad], axis=1)
    hidden2_grad, lowered = exchange(
        [],
        [
            ("tp", contract_last(pair_grad, pair_full).astype(jnp.bfloat16)),
            ("tp", contract_last(activation, wd_turned).astype(jnp.bfloat16)),
        ],
        5,
    )
    block_out = middle + lowered
    norm2_part = jnp.sum(hidden2_grad * normed_second, axis=0)
    middle_grad = norm_back(hidden2_grad * norm2_gain, normed_second, inv_second) + cotangent
    (mid_low,) = exchange([("tp", middle_grad.astype(jnp.bfloat16))], [], 6)
    attended_grad = jnp.dot(mid_low, wo_turned, preferred_element_type=jnp.float32).astype(
        jnp.bfloat16
    )
    delta_rows = jnp.sum(
        (attended_grad.astype(jnp.float32) * attended_flat.astype(jnp.float32)).reshape(
            block_len, local_heads, head_width
        ),
        axis=-1,
    )
    query_grad, key_terms = attention_call(
        attend_back_kernel,
        settings,
        (
            key_blocks,
            own_block,
            queries,
            all_keys,
            all_values,
            attended_grad,
            log_total.reshape(local_heads, 1, block_len),
            delta_rows.T.reshape(local_heads, 1, block_len),
        ),
        [
            jax.ShapeDtypeStruct((block_len, query_width), jnp.float32),
            jax.ShapeDtypeStruct((all_keys.shape[0], 2 * key_width), jnp.bfloat16),
        ],
        [],
    )
    query_grad = by_head(query_grad, head_width)
    (stacked_grads,) = exchange([], [("ctx", key_terms)], 7)
    key_grad = by_head(stacked_grads[:, :key_width], head_width)
    value_low = stacked_grads[:, key_width:].astype(jnp.bfloat16)
    query_back = rotate_back(query_grad, cosine, sine_table)
    q_gain_part = jnp.sum(query_back * query_hat, axis=(0, 1))
    query_raw_grad = by_row(
        norm_back(query_back * q_gain, query_hat, inv_query).astype(jnp.bfloat16)
    )
    key_back = rotate_back(key_grad, cosine, sine_table)
    k_gain_part = jnp.sum(key_back * key_hat, axis=(0, 1))
    key_raw_grad = by_row(norm_back(key_back * k_gain, key_hat, inv_key).astype(jnp.bfloat16))
    qkv_grad = jnp.concatenate([query_raw_grad, key_raw_grad, value_low], axis=1)
    (hidden1_grad,) = exchange(
        [], [("tp", contract_last(qkv_grad, qkv_full).astype(jnp.bfloat16))], 8
    )
    norm1_part = jnp.sum(hidden1_grad * normed_first, axis=0)
    input_grad = norm_back(hidden1_grad * norm1_gain, normed_first, inv_first) + middle_grad
    gain_parts = jnp.concatenate([norm1_part, norm2_part, q_gain_part, k_gain_part])
    gain_rows = -(-gain_parts.shape[0] // 1024) * 8
    gain_block = jnp.pad(gain_parts, (0, gain_rows * 128 - gain_parts.shape[0])).reshape(
        gain_rows, 128
    )
    (tp_gains,) = exchange([("tp", gain_block)], [], 9)
    gain_block = jnp.sum(tp_gains.reshape(-1, gain_rows, 128), axis=0)
    ctx_gains, qkv_wgrad, pair_wgrad, out_wgrad, down_wgrad = exchange(
        [("ctx", gain_block)],
        [
            ("ctx", contract_rows(hidden_first, qkv_grad).astype(jnp.bfloat16)),
            ("ctx", contract_rows(hidden_second, pair_grad).astype(jnp.bfloat16)),
            ("ctx", contract_rows(mid_low, attended_flat).astype(jnp.bfloat16)),
            ("ctx", contract_rows(cot_low, activation).astype(jnp.bfloat16)),
        ],
        10,
    )
    gains = jnp.sum(ctx_gains.reshape(-1, gain_rows, 128), axis=0).reshape(-1)
    width = norm1_gain.shape[0]
    return (
        block_out,
        input_grad,
        qkv_wgrad[:, :query_width],
        qkv_wgrad[:, query_width : query_width + key_width],
        qkv_wgrad[:, query_width + key_width :],
        out_wgrad.T,
        pair_wgrad[:, :unit_count],
        pair_wgrad[:, unit_count:],
        down_wgrad.T,
        gains[:width],
        gains[width : 2 * width],
        gains[2 * width : 2 * width + head_width],
        gains[2 * width + head_width : 2 * width + 2 * head_width],
    )


def solution(mesh):
    in_specs = (
        P(("ctx", "tp"), None),
        P("ctx"),
        P("ctx", "tp"),
        P("ctx", "tp"),
        P("ctx", "tp"),
        P("tp", "ctx"),
        P("ctx", "tp"),
        P("ctx", "tp"),
        P("tp", "ctx"),
        P(),
        P(),
        P(),
        P(),
        P(("ctx", "tp"), None),
    )
    out_specs = (
        P(("ctx", "tp"), None),
        P(("ctx", "tp"), None),
        P("ctx", "tp"),
        P("ctx", "tp"),
        P("ctx", "tp"),
        P("tp", "ctx"),
        P("ctx", "tp"),
        P("ctx", "tp"),
        P("tp", "ctx"),
        P(),
        P(),
        P(),
        P(),
    )
    return jax.shard_map(local, mesh=mesh, in_specs=in_specs, out_specs=out_specs, check_vma=False)
```
